32 devices in a mesh: sx: 16 (over z, x, core), sy: 2 (over y).
Axes of the slice: x: 2, y: 2, z: 4, core: 2. Of those that a mesh axis runs over, the one named last changes fastest.
Arguments:
- queries: bfloat16 [128, 5120], P('sx'), may hold values from -120 to 120
- cached_key_rows: bfloat16 [65536, 1024], P(('sx', 'sy')), may hold values from -6 to 6
- cached_value_rows: bfloat16 [65536, 1024], P(('sx', 'sy')), may hold values from -6 to 6
- stretch_opening_index: int32 [1], replicated, may hold values from 57344 to 65408
- valid_lengths: int32 [32], P(('sx', 'sy')), may hold values from 1024 to 2048, as said below
- out_weight: bfloat16 [5120, 5120], P('sy', 'sx'), may hold values from -0.078125 to 0.078125
Outputs:
- output: bfloat16 [128, 5120], P('sy', 'sx')
The draws below stay inside these ranges and needn't reach their ends.
Inputs may be any that keep to these rules, and one draw needn't show every extreme that they name: `valid_lengths`: some block is full in every draw.
All inputs are finite; a program needn't handle non-finite values.
Results may differ from the reference program's by a relative error of at most 0.0049.
Values may be sent and summed in bfloat16 or wider, within the bound.
A program may use at most 128 MiB of HBM per device.

```python
import jax
import jax.numpy as jnp
from jax import lax

D = 5120
HQ = 40
KEY_VALUE_HEADS = 8
HEAD_SIZE = 128
QUERY_GROUP_SIZE = 5
SPAN_TOKENS = 128
CACHE_PER_DEVICE = 2048
CACHE_POSITIONS = 65536


def draw_cached_key_rows(key, part):
    key = jax.random.fold_in(key, 3)
    base_position = jnp.clip(jax.random.normal(key, (CACHE_POSITIONS, KEY_VALUE_HEADS * HEAD_SIZE), jnp.float32), -6.0, 6.0)
    return base_position.astype(jnp.bfloat16)


def draw_queries(key, part):
    key = jax.random.fold_in(key, 4)
    base_position = 3.0 * jnp.clip(jax.random.normal(key, (SPAN_TOKENS, HQ * HEAD_SIZE), jnp.float32), -6.0, 6.0)
    return base_position.astype(jnp.bfloat16)


def draw_valid_lengths(key, part):
    key = jax.random.fold_in(key, 5)
    count_of_blocks = CACHE_POSITIONS // CACHE_PER_DEVICE
    lengths = jax.random.randint(key, (count_of_blocks,), CACHE_PER_DEVICE // 2, CACHE_PER_DEVICE + 1)
    full_block = jax.random.randint(jax.random.fold_in(key, 6), (), 0, count_of_blocks)
    return lengths.at[full_block].set(CACHE_PER_DEVICE).astype(jnp.int32)


def shard_levels(stream_key, shape, split, least, high):
    def one(position, shards_of):
        heights = jax.random.uniform(jax.random.fold_in(jax.random.fold_in(stream_key, 6), position), (shards_of,), jnp.float32, least / len(split), high / len(split))
        return jnp.repeat(jnp.exp(heights), shape[position] // shards_of).reshape((-1,) + (1,) * (len(shape) - position - 1))

    factor_of = one(*split[0])
    for cut in split[1:]:
        factor_of = factor_of * one(*cut)
    return factor_of


def centred(rng, dims, width, most, cuts=(), kind=jnp.bfloat16):
    drawn = jax.random.normal(rng, dims, jnp.float32) * width
    if len(cuts) > 0:
        drawn = shard_levels(rng, dims, cuts, -0.22, 0.18) * drawn
    return jnp.clip(drawn, min=-most, max=most).astype(kind)


def setup_inputs(seed: int = 0) -> dict:
    key_of = jax.random.split(jax.random.key(seed), 7)
    queries = draw_queries(jax.random.fold_in(key_of[6], 71), 0)
    cached_key_rows = draw_cached_key_rows(jax.random.fold_in(key_of[6], 71), 0)
    cached_value_rows = centred(key_of[2], (CACHE_POSITIONS, KEY_VALUE_HEADS * HEAD_SIZE), 1.0, 6.0, ((0, 32),))
    stretch_opening_index = jax.random.randint(key_of[3], (1,), CACHE_POSITIONS - 4 * CACHE_PER_DEVICE, CACHE_POSITIONS - SPAN_TOKENS + 1).astype(jnp.int32)
    valid_lengths = draw_valid_lengths(jax.random.fold_in(key_of[6], 71), 0)
    out_weight = centred(key_of[5], (HQ * HEAD_SIZE, D), (HQ * HEAD_SIZE) ** -0.5, 0.078125, ((0, 2), (1, 16)))
    return {"queries": queries, "cached_key_rows": cached_key_rows, "cached_value_rows": cached_value_rows, "stretch_opening_index": stretch_opening_index, "valid_lengths": valid_lengths, "out_weight": out_weight}


def normalizer_divisor(stretch_opening_index):
    positions = stretch_opening_index[0] + jnp.arange(SPAN_TOKENS, dtype=jnp.int32)
    buckets = ((positions + 1) // 8192).astype(jnp.float32)
    return (1.0 + 0.1 * jnp.log(buckets + 1.0)) * (HEAD_SIZE ** -0.5)


def reference(queries, cached_key_rows, cached_value_rows, stretch_opening_index, valid_lengths, out_weight):
    count_of_blocks = CACHE_POSITIONS // CACHE_PER_DEVICE
    heads_of_query = queries.astype(jnp.float32).reshape(SPAN_TOKENS, KEY_VALUE_HEADS, QUERY_GROUP_SIZE, HEAD_SIZE)
    score_multiplier = normalizer_divisor(stretch_opening_index)
    query_positions = stretch_opening_index[0] + jnp.arange(SPAN_TOKENS, dtype=jnp.int32)
    blocked_keys = cached_key_rows.reshape(count_of_blocks, CACHE_PER_DEVICE, KEY_VALUE_HEADS, HEAD_SIZE)
    blocked_values = cached_value_rows.reshape(count_of_blocks, CACHE_PER_DEVICE, KEY_VALUE_HEADS, HEAD_SIZE)
    block_ids = jnp.arange(count_of_blocks, dtype=jnp.int32)

    def visit(carry, inputs):
        running_max, running_out, running_total = carry
        key_block, value_block, extent_along, block_id = inputs
        scores = jnp.einsum("tgid,cgd->tgic", heads_of_query, key_block.astype(jnp.float32))
        scores = scores * score_multiplier[:, None, None, None]
        entry_indices = jnp.arange(CACHE_PER_DEVICE, dtype=jnp.int32)
        key_positions = block_id * CACHE_PER_DEVICE + entry_indices
        visible = (entry_indices < extent_along)[None, :] & (key_positions[None, :] <= query_positions[:, None])
        seen_mask = visible[:, None, None, :]
        scores = jnp.where(seen_mask, scores, -1e30)
        block_max = jnp.max(scores, axis=-1)
        weights = jnp.where(seen_mask, jnp.exp(scores - block_max[..., None]), 0.0)
        block_total = jnp.sum(weights, axis=-1)
        rounded = lax.optimization_barrier(weights.astype(jnp.bfloat16))
        block_out = jnp.einsum("tgic,cgd->tgid", rounded.astype(jnp.float32), value_block.astype(jnp.float32))
        updated_peak = jnp.maximum(running_max, block_max)
        old_factor = jnp.exp(running_max - updated_peak)
        new_factor = jnp.exp(block_max - updated_peak)
        running_out = running_out * old_factor[..., None] + block_out * new_factor[..., None]
        running_total = running_total * old_factor + block_total * new_factor
        return (updated_peak, running_out, running_total), None

    initial_state = (jnp.full((SPAN_TOKENS, KEY_VALUE_HEADS, QUERY_GROUP_SIZE), -1e30, jnp.float32),
                   jnp.zeros((SPAN_TOKENS, KEY_VALUE_HEADS, QUERY_GROUP_SIZE, HEAD_SIZE), jnp.float32),
                   jnp.zeros((SPAN_TOKENS, KEY_VALUE_HEADS, QUERY_GROUP_SIZE), jnp.float32))
    final_carry, unused = lax.scan(visit, initial_state, (blocked_keys, blocked_values, valid_lengths, block_ids))
    summed = final_carry[1]
    total = final_carry[2]
    attended = (summed / total[..., None]).reshape(SPAN_TOKENS, HQ * HEAD_SIZE).astype(jnp.bfloat16)
    return jnp.dot(attended, out_weight, preferred_element_type=jnp.float32).astype(jnp.bfloat16)
```

```python
import functools
import math

import jax
import jax.numpy as jnp
from jax import lax
from jax.experimental import pallas as pl
from jax.experimental.pallas import tpu as pltpu
from jax.sharding import PartitionSpec as P

HEAD = 128
KV = 8
GROUP = 5
PIECE = 8
ROWS = 48
F32 = jnp.float32
BF16 = jnp.bfloat16
MESH = pl.DeviceIdType.MESH
LOG2E = math.log2(math.e)


def wait_for(ref, sem):
    pltpu.make_async_copy(ref, ref, sem).wait()


def kernel(
    nsx, nsy,
    q_ref, k_hbm, v_hbm, open_ref, valid_ref, w_hbm, out_ref,
    kbuf, vbuf, wbuf, qg, qf, bias, temper, obuf, stat, crecv, cstat,
    dsend, drecv, ag, att, acc, ysend, yrecv,
    ksem, vsem, wsem, qd_s, qd_r, qc_s, qc_r, c_s, c_r, t_s, t_r,
    d_s, d_r, a_s, a_r, f_s, f_r, y_s, y_r,
):
    np_ = nsx // 2
    nch = KV // nsy
    heads = nsy * GROUP
    tokens = qf.shape[1]
    half = tokens // 2
    slots = kbuf.shape[1]
    owners = half // PIECE
    tb = tokens // nsx
    sx = lax.axis_index("sx")
    sy = lax.axis_index("sy")
    core = lax.rem(sx, 2)
    other = 1 - core
    p = sx // 2
    grp = (p // owners) * owners
    lane_p = lax.rem(p, owners)
    partner = {"sx": p * 2 + other, "sy": sy}

    def same_core(i):
        at = lax.rem(sy * np_ + p + i, np_ * nsy)
        return {"sx": lax.rem(at, np_) * 2 + core, "sy": at // np_}, at

    barrier = pltpu.get_barrier_semaphore()

    def greet(i, _):
        dev, _at = same_core(i)
        pl.semaphore_signal(barrier, inc=1, device_id=dev, device_id_type=MESH)
        return 0

    lax.fori_loop(1, np_ * nsy, greet, 0)
    pl.semaphore_signal(barrier, inc=1, device_id=partner, device_id_type=MESH)

    order = [j * nch + c for c in range(nch) for j in range(nsy)]

    def load_k(g):
        return pltpu.make_async_copy(k_hbm.at[:, pl.ds(g * HEAD, HEAD)], kbuf.at[g], ksem.at[g])

    def load_v(g):
        return pltpu.make_async_copy(
            v_hbm.at[:, pl.ds(g * HEAD, HEAD)], vbuf.at[g, :, pl.ds(0, HEAD)], vsem.at[g])

    for g in order:
        load_k(g).start()
        load_v(g).start()
    load_w = pltpu.make_async_copy(w_hbm, wbuf, wsem)
    load_w.start()

    pl.semaphore_wait(barrier, np_ * nsy)

    for c in range(nch):
        def send_q(i, _, c=c):
            to = lax.rem(p + i, np_)
            pltpu.make_async_remote_copy(
                q_ref.at[c], qg.at[c, core, p], qd_s.at[c], qd_r.at[c],
                device_id={"sx": to * 2 + core, "sy": sy}, device_id_type=MESH).start()
            return 0
        lax.fori_loop(1, np_, send_q, 0)
        qg[c, core, p] = q_ref[c]

    t_col = lax.broadcasted_iota(jnp.int32, (tokens, 1), 0)
    position = open_ref[0] + t_col
    buckets = lax.shift_right_logical(position + 1, 13).astype(F32)
    temper[...] = jnp.broadcast_to(
        (1.0 + 0.1 * jnp.log(buckets + 1.0)) * (HEAD ** -0.5 * LOG2E), temper.shape)
    limit = jnp.minimum(valid_ref[0], position + 1 - (sx * nsy + sy) * slots)
    bias[...] = jnp.where(
        lax.broadcasted_iota(jnp.int32, (tokens, slots), 1) < limit, 0.0, -1e30).astype(F32)

    def ones(g, _):
        vbuf[g, :, HEAD:] = jnp.ones((slots, HEAD), BF16)
        return 0
    lax.fori_loop(0, KV, ones, 0)
    acc[...] = jnp.zeros_like(acc)

    def forward_q(c):
        wait_for(qg.at[c, 0, pl.ds(0, np_ - 1)], qd_r.at[c])
        pltpu.make_async_remote_copy(
            qg.at[c, core], qg.at[c, core], qc_s.at[c], qc_r.at[c],
            device_id=partner, device_id_type=MESH).start()

    def take_q(c):
        wait_for(qg.at[c, 0], qc_r.at[c])

        def place(i, _):
            x0 = qg[c, 0, i].astype(F32)
            x1 = qg[c, 1, i].astype(F32)
            at = pl.multiple_of(i * 2 * tb, 2 * tb)
            for k in range(heads):
                qf[k, pl.ds(at, 2 * tb), :] = jnp.concatenate(
                    [x0[k * tb:(k + 1) * tb], x1[k * tb:(k + 1) * tb]], axis=0)
            return 0
        lax.fori_loop(0, np_, place, 0)
        stat[c, :, 0] = jnp.full((2, half, HEAD), -1e29, F32)
        stat[c, :, 1] = jnp.zeros((2, half, HEAD), F32)

    def attend(c, j):
        g = j * nch + c
        load_k(g).wait()
        load_v(g).wait()

        def one(h, _):
            k = j * GROUP + h
            s = lax.dot_general(qf[k].astype(BF16), kbuf[g], (((1,), (1,)), ((), ())),
                                preferred_element_type=F32)
            s = s * temper[:, :1] + bias[...]
            m = jnp.maximum(jnp.max(s, axis=1, keepdims=True), -1e29).astype(BF16).astype(F32)
            w = jnp.exp2(s - m).astype(BF16)
            o = jnp.dot(w, vbuf[g], preferred_element_type=F32)
            lane = lax.broadcasted_iota(jnp.int32, (half, HEAD), 1) == k
            for b in range(2):
                rows = slice(b * half, (b + 1) * half)
                obuf[c, b, k] = o[rows, :HEAD].astype(BF16)
                stat[c, b, 0] = jnp.where(lane, m[rows], stat[c, b, 0])
                stat[c, b, 1] = jnp.where(lane, o[rows, HEAD:], stat[c, b, 1])
            return 0
        lax.fori_loop(0, GROUP, one, 0)

    def pair_copies(c):
        return (
            pltpu.make_async_remote_copy(
                obuf.at[c, other], crecv.at[c], c_s.at[c], c_r.at[c],
                device_id=partner, device_id_type=MESH),
            pltpu.make_async_remote_copy(
                stat.at[c, other], cstat.at[c], t_s.at[c], t_r.at[c],
                device_id=partner, device_id_type=MESH))

    def send_pair(c):
        for copy in pair_copies(c):
            copy.start()

    def send_owners(c):
        for copy in pair_copies(c):
            copy.wait_recv()
        m0, m1 = stat[c, core, 0], cstat[c, 0]
        m = jnp.maximum(m0, m1)
        f0, f1 = jnp.exp2(m0 - m), jnp.exp2(m1 - m)
        l = stat[c, core, 1] * f0 + cstat[c, 1] * f1
        hi = l.astype(BF16).astype(F32)
        lo = l - hi
        lane = lax.broadcasted_iota(jnp.int32, (half, HEAD), 1)
        for j in range(nsy):
            def turn(x, by):
                by = by % HEAD
                return pltpu.roll(x, by, 1) if by else x
            st = jnp.where(lane < 8, turn(m, -GROUP * j),
                           jnp.where(lane < 16, turn(hi, 8 - GROUP * j), turn(lo, 16 - GROUP * j)))
            parts = []
            for h in range(GROUP):
                k = j * GROUP + h
                parts.append(obuf[c, core, k].astype(F32) * f0[:, k:k + 1]
                             + crecv[c, k].astype(F32) * f1[:, k:k + 1])
            parts.append(st)
            for o in range(owners):
                rows = slice(o * PIECE, (o + 1) * PIECE)
                dsend[c, j, o] = jnp.concatenate([x[rows] for x in parts], axis=0).astype(BF16)
        here = sy * np_ + p
        drecv[c, here] = dsend[c, sy, lane_p]

        def send(i, _):
            dev, at = same_core(i)
            pltpu.make_async_remote_copy(
                dsend.at[c, at // np_, lax.rem(at, owners)], drecv.at[c, here], d_s.at[c], d_r.at[c],
                device_id=dev, device_id_type=MESH).start()
            return 0
        lax.fori_loop(1, np_ * nsy, send, 0)

    def send_attended(c):
        n = np_ * nsy
        wait_for(drecv.at[c, pl.ds(0, n - 1)], d_r.at[c])
        first = GROUP * PIECE

        def largest(i, m):
            return jnp.maximum(m, drecv[c, i].astype(F32)[first:])
        m = lax.fori_loop(0, n, largest, jnp.full((PIECE, HEAD), -1e29, F32))

        def add(i, carry):
            x = drecv[c, i].astype(F32)
            st = x[first:]
            f = jnp.exp2(st - m)
            l = pltpu.roll(st, HEAD - 8, 1) + pltpu.roll(st, HEAD - 16, 1)
            outs = tuple(
                a + f[:, h:h + 1] * x[h * PIECE:(h + 1) * PIECE] for h, a in enumerate(carry[1:]))
            return (carry[0] + f * l,) + outs
        zero = jnp.zeros((PIECE, HEAD), F32)
        total, *outs = lax.fori_loop(0, n, add, (zero,) * (GROUP + 1))
        outs = [o / total[:, h:h + 1] for h, o in enumerate(outs)]
        ag[c, core, lane_p] = jnp.concatenate(outs + [zero], axis=0).astype(BF16)

        def send(i, _):
            to = grp + lax.rem(lane_p + i, owners)
            pltpu.make_async_remote_copy(
                ag.at[c, core, lane_p], ag.at[c, core, lane_p], a_s.at[c], a_r.at[c],
                device_id={"sx": to * 2 + core, "sy": sy}, device_id_type=MESH).start()
            return 0
        lax.fori_loop(1, owners, send, 0)

    def forward_attended(c):
        wait_for(ag.at[c, 0, pl.ds(0, owners - 1)], a_r.at[c])
        pltpu.make_async_remote_copy(
            ag.at[c, core], ag.at[c, core], f_s.at[c], f_r.at[c],
            device_id=partner, device_id_type=MESH).start()

    def project(c):
        wait_for(ag.at[c, 0], f_r.at[c])
        if c == 0:
            load_w.wait()
        for b in range(2):
            for o in range(owners):
                x = ag[c, b, o].astype(F32)
                for h in range(GROUP):
                    att[pl.ds(b * half + o * PIECE, PIECE), pl.ds(h * HEAD, HEAD)] = (
                        x[h * PIECE:(h + 1) * PIECE])
        width = GROUP * HEAD
        acc[...] += jnp.dot(att[...].astype(BF16), wbuf[pl.ds(c * width, width), :],
                            preferred_element_type=F32)

    forward_q(0)
    stages = (send_pair, send_owners, send_attended, forward_attended, project)
    for step in range(2 * nch + 4):
        c = step // 2
        if step % 2 == 0 and c < nch:
            take_q(c)
        if c < nch:
            split = (nsy + 1) // 2
            for j in (range(split) if step % 2 == 0 else range(split, nsy)):
                attend(c, j)
        if step % 2 == 0 and c + 1 < nch:
            forward_q(c + 1)
        for s, stage in enumerate(stages):
            at = step - 1 - s
            if at >= 0 and at % 2 == 0 and at // 2 < nch:
                stage(at // 2)

    block = tokens // nsy
    for j in range(nsy):
        ysend[j] = acc[j * block:(j + 1) * block, :]

    def send_y(i, _):
        to = lax.rem(sy + i, nsy)
        pltpu.make_async_remote_copy(
            ysend.at[to], yrecv.at[sy], y_s, y_r,
            device_id={"sx": sx, "sy": to}, device_id_type=MESH).start()
        return 0
    lax.fori_loop(1, nsy, send_y, 0)
    yrecv[sy] = ysend[sy]
    wait_for(yrecv.at[pl.ds(0, nsy - 1)], y_r)
    total = yrecv[0]
    for j in range(1, nsy):
        total = total + yrecv[j]
    out_ref[...] = total.astype(BF16)

    wait_for(ysend.at[pl.ds(0, nsy - 1)], y_s)
    for c in range(nch):
        wait_for(qg.at[c, 0, pl.ds(0, np_ - 1)], qd_s.at[c])
        wait_for(qg.at[c, 0], qc_s.at[c])
        for copy in pair_copies(c):
            copy.wait_send()
        wait_for(drecv.at[c, pl.ds(0, np_ * nsy - 1)], d_s.at[c])
        wait_for(ag.at[c, 0, pl.ds(0, owners - 1)], a_s.at[c])
        wait_for(ag.at[c, 0], f_s.at[c])


def solution(mesh):
    nsx, nsy = mesh.shape["sx"], mesh.shape["sy"]
    nch = KV // nsy
    heads = nsy * GROUP
    np_ = nsx // 2

    def per_device(queries, keys, values, opening, valid, weight):
        tb = queries.shape[0]
        tokens = tb * nsx
        half = tokens // 2
        owners = half // PIECE
        slots = keys.shape[0]
        q = queries.reshape(tb, nsy, nch, GROUP, HEAD).transpose(2, 1, 3, 0, 4)
        q = q.reshape(nch, heads * tb, HEAD)
        columns = weight.shape[1]
        dma = pltpu.SemaphoreType.DMA
        vmem = pl.BlockSpec(memory_space=pltpu.VMEM)
        smem = pl.BlockSpec(memory_space=pltpu.SMEM)
        hbm = pl.BlockSpec(memory_space=pl.ANY)
        return pl.pallas_call(
            functools.partial(kernel, nsx, nsy),
            out_shape=jax.ShapeDtypeStruct((tokens // nsy, columns), BF16),
            in_specs=[vmem, hbm, hbm, smem, smem, hbm],
            out_specs=vmem,
            scratch_shapes=[
                pltpu.VMEM((KV, slots, HEAD), BF16),
                pltpu.VMEM((KV, slots, 2 * HEAD), BF16),
                pltpu.VMEM(weight.shape, BF16),
                pltpu.VMEM((nch, 2, np_, heads * tb, HEAD), BF16),
                pltpu.VMEM((heads, tokens, HEAD), F32),
                pltpu.VMEM((tokens, slots), F32),
                pltpu.VMEM((tokens, HEAD), F32),
                pltpu.VMEM((nch, 2, heads, half, HEAD), BF16),
                pltpu.VMEM((nch, 2, 2, half, HEAD), F32),
                pltpu.VMEM((nch, heads, half, HEAD), BF16),
                pltpu.VMEM((nch, 2, half, HEAD), F32),
                pltpu.VMEM((nch, nsy, owners, ROWS, HEAD), BF16),
                pltpu.VMEM((nch, np_ * nsy, ROWS, HEAD), BF16),
                pltpu.VMEM((nch, 2, owners, ROWS, HEAD), BF16),
                pltpu.VMEM((tokens, GROUP * HEAD), F32),
                pltpu.VMEM((tokens, columns), F32),
                pltpu.VMEM((nsy, tokens // nsy, columns), F32),
                pltpu.VMEM((nsy, tokens // nsy, columns), F32),
                dma((KV,)), dma((KV,)), dma,
            ] + [dma((nch,))] * 14 + [dma, dma],
            compiler_params=pltpu.CompilerParams(
                collective_id=0, has_side_effects=True, vmem_limit_bytes=56 * 1024 * 1024),
        )(q, keys, values, opening, valid, weight)

    return jax.shard_map(
        per_device,
        mesh=mesh,
        in_specs=(
            P("sx", None),
            P(("sx", "sy"), None),
            P(("sx", "sy"), None),
            P(),
            P(("sx", "sy")),
            P("sy", "sx"),
        ),
        out_specs=P("sy", "sx"),
        check_vma=False,
    )
```

```python
import functools
import math

import jax
import jax.numpy as jnp
from jax import lax
from jax.experimental import pallas as pl
from jax.experimental.pallas import tpu as pltpu
from jax.sharding import PartitionSpec as P

HEAD = 128
KV = 8
GROUP = 5
BLOCK = 512
PIECE = 8
ROWS = 48
F32 = jnp.float32
BF16 = jnp.bfloat16
MESH = pl.DeviceIdType.MESH
LOG2E = math.log2(math.e)


def wait_for(ref, sem):
    pltpu.make_async_copy(ref, ref, sem).wait()


def kernel(
    nsx, nsy,
    q_ref, k_hbm, v_hbm, open_ref, valid_ref, w_hbm, out_ref,
    kbuf, vbuf, wbuf, qg, qf, qb, bias, temper, score0, score1, top0, top1, part, oacc, obuf, stat, crecv, cstat,
    dsend, drecv, ag, att, acc, ysend, yrecv,
    ksem, vsem, wsem, qd_s, qd_r, qc_s, qc_r, c_s, c_r, t_s, t_r,
    d_s, d_r, a_s, a_r, f_s, f_r, y_s, y_r,
):
    np_ = nsx // 2
    nch = KV // nsy
    heads = nsy * GROUP
    tokens = qf.shape[1]
    half = tokens // 2
    slots = kbuf.shape[1]
    owners = half // PIECE
    tb = tokens // nsx
    sx = lax.axis_index("sx")
    sy = lax.axis_index("sy")
    core = lax.rem(sx, 2)
    other = 1 - core
    p = sx // 2
    grp = (p // owners) * owners
    lane_p = lax.rem(p, owners)
    partner = {"sx": p * 2 + other, "sy": sy}

    def same_core(i):
        at = lax.rem(sy * np_ + p + i, np_ * nsy)
        return {"sx": lax.rem(at, np_) * 2 + core, "sy": at // np_}, at

    barrier = pltpu.get_barrier_semaphore()

    def greet(i, _):
        dev, _at = same_core(i)
        pl.semaphore_signal(barrier, inc=1, device_id=dev, device_id_type=MESH)
        return 0

    lax.fori_loop(1, np_ * nsy, greet, 0)
    pl.semaphore_signal(barrier, inc=1, device_id=partner, device_id_type=MESH)

    order = [j * nch + c for c in range(nch) for j in range(nsy)]

    def load_k(g):
        return pltpu.make_async_copy(k_hbm.at[:, pl.ds(g * HEAD, HEAD)], kbuf.at[g], ksem.at[g])

    def load_v(g):
        return pltpu.make_async_copy(
            v_hbm.at[:, pl.ds(g * HEAD, HEAD)], vbuf.at[g, :, pl.ds(0, HEAD)], vsem.at[g])

    for g in order:
        load_k(g).start()
        load_v(g).start()
    load_w = pltpu.make_async_copy(w_hbm, wbuf, wsem)
    load_w.start()

    pl.semaphore_wait(barrier, np_ * nsy)

    for c in range(nch):
        def send_q(i, _, c=c):
            to = lax.rem(p + i, np_)
            pltpu.make_async_remote_copy(
                q_ref.at[c], qg.at[c, core, p], qd_s.at[c], qd_r.at[c],
                device_id={"sx": to * 2 + core, "sy": sy}, device_id_type=MESH).start()
            return 0
        lax.fori_loop(1, np_, send_q, 0)
        qg[c, core, p] = q_ref[c]

    t_col = lax.broadcasted_iota(jnp.int32, (tokens, 1), 0)
    position = open_ref[0] + t_col
    buckets = lax.shift_right_logical(position + 1, 13).astype(F32)
    temper[...] = jnp.broadcast_to(
        (1.0 + 0.1 * jnp.log(buckets + 1.0)) * (HEAD ** -0.5 * LOG2E), temper.shape)
    limit = jnp.minimum(valid_ref[0], position + 1 - (sx * nsy + sy) * slots)
    bias[...] = jnp.where(
        lax.broadcasted_iota(jnp.int32, (tokens, slots), 1) < limit, 0.0, -1e30).astype(F32)

    def ones(g, _):
        vbuf[g, :, HEAD:] = jnp.ones((slots, HEAD), BF16)
        return 0
    lax.fori_loop(0, KV, ones, 0)
    acc[...] = jnp.zeros_like(acc)

    def forward_q(c):
        wait_for(qg.at[c, 0, pl.ds(0, np_ - 1)], qd_r.at[c])
        pltpu.make_async_remote_copy(
            qg.at[c, core], qg.at[c, core], qc_s.at[c], qc_r.at[c],
            device_id=partner, device_id_type=MESH).start()

    def take_q(c):
        wait_for(qg.at[c, 0], qc_r.at[c])

        def place(i, _):
            x0 = qg[c, 0, i].astype(F32)
            x1 = qg[c, 1, i].astype(F32)
            at = pl.multiple_of(i * 2 * tb, 2 * tb)
            for k in range(heads):
                qf[k, pl.ds(at, 2 * tb), :] = jnp.concatenate(
                    [x0[k * tb:(k + 1) * tb], x1[k * tb:(k + 1) * tb]], axis=0)
            return 0
        lax.fori_loop(0, np_, place, 0)
        stat[c, :, 0] = jnp.full((2, half, HEAD), -1e29, F32)
        stat[c, :, 1] = jnp.zeros((2, half, HEAD), F32)

    scores, tops = (score0, score1), (top0, top1)

    def wide(x):
        return jnp.concatenate([x] * (BLOCK // HEAD), axis=1)

    def step(cur, nxt):
        if nxt is not None:
            g = order[nxt]
            load_k(g).wait()
            first = (nxt % nsy) * GROUP
            for h in range(GROUP):
                qb[pl.ds(h * tokens, tokens), :] = qf[first + h].astype(BF16)
            part[...] = jnp.full(part.shape, -1e29, F32)
        if cur is not None:
            load_v(order[cur]).wait()
            oacc[...] = jnp.zeros_like(oacc)

        def block(n, _):
            at = pl.multiple_of(n * BLOCK, BLOCK)
            keys = pl.ds(at, BLOCK)
            if nxt is not None:
                s = lax.dot_general(qb[...], kbuf[order[nxt], keys, :], (((1,), (1,)), ((), ())),
                                    preferred_element_type=F32)
                scale, hide = wide(temper[...]), bias[:, keys]
                for h in range(GROUP):
                    rows = slice(h * tokens, (h + 1) * tokens)
                    x = s[rows] * scale + hide
                    scores[nxt % 2][rows, keys] = x
                    m = part[rows, :]
                    for i in range(BLOCK // HEAD):
                        m = jnp.maximum(m, x[:, i * HEAD:(i + 1) * HEAD])
                    part[rows, :] = m
            if cur is not None:
                w = jnp.exp2(scores[cur % 2][:, keys] - wide(tops[cur % 2][...])).astype(BF16)
                oacc[...] += jnp.dot(w, vbuf[order[cur], keys, :], preferred_element_type=F32)
            return 0
        lax.fori_loop(0, slots // BLOCK, block, 0)

        if nxt is not None:
            tops[nxt % 2][...] = jnp.broadcast_to(
                jnp.max(part[...], axis=1, keepdims=True), part.shape)
        if cur is not None:
            c = cur // nsy
            lane = lax.broadcasted_iota(jnp.int32, (half, HEAD), 1)
            for b in range(2):
                m, l = stat[c, b, 0], stat[c, b, 1]
                for h in range(GROUP):
                    k = (cur % nsy) * GROUP + h
                    rows = pl.ds(h * tokens + b * half, half)
                    obuf[c, b, k] = oacc[rows, :HEAD].astype(BF16)
                    m = jnp.where(lane == k, tops[cur % 2][rows, :], m)
                    l = jnp.where(lane == k, oacc[rows, HEAD:], l)
                stat[c, b, 0], stat[c, b, 1] = m, l

    def pair_copies(c):
        return (
            pltpu.make_async_remote_copy(
                obuf.at[c, other], crecv.at[c], c_s.at[c], c_r.at[c],
                device_id=partner, device_id_type=MESH),
            pltpu.make_async_remote_copy(
                stat.at[c, other], cstat.at[c], t_s.at[c], t_r.at[c],
                device_id=partner, device_id_type=MESH))

    def send_pair(c):
        for copy in pair_copies(c):
            copy.start()

    def send_owners(c):
        for copy in pair_copies(c):
            copy.wait_recv()
        m0, m1 = stat[c, core, 0], cstat[c, 0]
        m = jnp.maximum(m0, m1)
        f0, f1 = jnp.exp2(m0 - m), jnp.exp2(m1 - m)
        l = stat[c, core, 1] * f0 + cstat[c, 1] * f1
        terms = []
        for x, n in ((m, 3), (l, 2)):
            for _ in range(n):
                terms.append(x.astype(BF16).astype(F32))
                x = x - terms[-1]
        lane = lax.broadcasted_iota(jnp.int32, (half, HEAD), 1)
        for j in range(nsy):
            def turn(x, by):
                by = by % HEAD
                return pltpu.roll(x, by, 1) if by else x
            st = turn(terms[0], -GROUP * j)
            for i in range(1, len(terms)):
                st = jnp.where(lane < 8 * i, st, turn(terms[i], 8 * i - GROUP * j))
            parts = []
            for h in range(GROUP):
                k = j * GROUP + h
                parts.append(obuf[c, core, k].astype(F32) * f0[:, k:k + 1]
                             + crecv[c, k].astype(F32) * f1[:, k:k + 1])
            parts.append(st)
            for o in range(owners):
                rows = slice(o * PIECE, (o + 1) * PIECE)
                dsend[c, j, o] = jnp.concatenate([x[rows] for x in parts], axis=0).astype(BF16)
        here = sy * np_ + p
        drecv[c, here] = dsend[c, sy, lane_p]

        def send(i, _):
            dev, at = same_core(i)
            pltpu.make_async_remote_copy(
                dsend.at[c, at // np_, lax.rem(at, owners)], drecv.at[c, here], d_s.at[c], d_r.at[c],
                device_id=dev, device_id_type=MESH).start()
            return 0
        lax.fori_loop(1, np_ * nsy, send, 0)

    def send_attended(c):
        n = np_ * nsy
        wait_for(drecv.at[c, pl.ds(0, n - 1)], d_r.at[c])
        first = GROUP * PIECE

        def join(st, *at):
            return sum(pltpu.roll(st, HEAD - 8 * i, 1) for i in at)

        def largest(i, m):
            st = drecv[c, i].astype(F32)[first:]
            return jnp.maximum(m, st + join(st, 1, 2))
        m = lax.fori_loop(0, n, largest, jnp.full((PIECE, HEAD), -1e29, F32))

        def add(i, carry):
            x = drecv[c, i].astype(F32)
            st = x[first:]
            f = jnp.exp2(st + join(st, 1, 2) - m)
            l = join(st, 3, 4)
            outs = tuple(
                a + f[:, h:h + 1] * x[h * PIECE:(h + 1) * PIECE] for h, a in enumerate(carry[1:]))
            return (carry[0] + f * l,) + outs
        zero = jnp.zeros((PIECE, HEAD), F32)
        total, *outs = lax.fori_loop(0, n, add, (zero,) * (GROUP + 1))
        outs = [o / total[:, h:h + 1] for h, o in enumerate(outs)]
        ag[c, core, lane_p] = jnp.concatenate(outs + [zero], axis=0).astype(BF16)

        def send(i, _):
            to = grp + lax.rem(lane_p + i, owners)
            pltpu.make_async_remote_copy(
                ag.at[c, core, lane_p], ag.at[c, core, lane_p], a_s.at[c], a_r.at[c],
                device_id={"sx": to * 2 + core, "sy": sy}, device_id_type=MESH).start()
            return 0
        lax.fori_loop(1, owners, send, 0)

    def forward_attended(c):
        wait_for(ag.at[c, 0, pl.ds(0, owners - 1)], a_r.at[c])
        pltpu.make_async_remote_copy(
            ag.at[c, core], ag.at[c, core], f_s.at[c], f_r.at[c],
            device_id=partner, device_id_type=MESH).start()

    def project(c):
        wait_for(ag.at[c, 0], f_r.at[c])
        if c == 0:
            load_w.wait()
        for b in range(2):
            for o in range(owners):
                x = ag[c, b, o].astype(F32)
                for h in range(GROUP):
                    att[pl.ds(b * half + o * PIECE, PIECE), pl.ds(h * HEAD, HEAD)] = (
                        x[h * PIECE:(h + 1) * PIECE])
        width = GROUP * HEAD
        acc[...] += jnp.dot(att[...].astype(BF16), wbuf[pl.ds(c * width, width), :],
                            preferred_element_type=F32)

    stages = (send_pair, send_owners, send_attended, forward_attended, project)
    forward_q(0)
    take_q(0)
    step(None, 0)
    for i in range(KV + len(stages) - 1):
        if i % nsy == 0 and i // nsy + 1 < nch:
            forward_q(i // nsy + 1)
        if (i + 1) % nsy == 0 and (i + 1) // nsy < nch:
            take_q((i + 1) // nsy)
        if i < KV:
            step(i, i + 1 if i + 1 < KV else None)
        for s, stage in enumerate(stages):
            done = i + 1 - s
            if done % nsy == 0 and 0 < done <= KV:
                stage(done // nsy - 1)

    block = tokens // nsy
    for j in range(nsy):
        ysend[j] = acc[j * block:(j + 1) * block, :]

    def send_y(i, _):
        to = lax.rem(sy + i, nsy)
        pltpu.make_async_remote_copy(
            ysend.at[to], yrecv.at[sy], y_s, y_r,
            device_id={"sx": sx, "sy": to}, device_id_type=MESH).start()
        return 0
    lax.fori_loop(1, nsy, send_y, 0)
    yrecv[sy] = ysend[sy]
    wait_for(yrecv.at[pl.ds(0, nsy - 1)], y_r)
    total = yrecv[0]
    for j in range(1, nsy):
        total = total + yrecv[j]
    out_ref[...] = total.astype(BF16)

    wait_for(ysend.at[pl.ds(0, nsy - 1)], y_s)
    for c in range(nch):
        wait_for(qg.at[c, 0, pl.ds(0, np_ - 1)], qd_s.at[c])
        wait_for(qg.at[c, 0], qc_s.at[c])
        for copy in pair_copies(c):
            copy.wait_send()
        wait_for(drecv.at[c, pl.ds(0, np_ * nsy - 1)], d_s.at[c])
        wait_for(ag.at[c, 0, pl.ds(0, owners - 1)], a_s.at[c])
        wait_for(ag.at[c, 0], f_s.at[c])


def solution(mesh):
    nsx, nsy = mesh.shape["sx"], mesh.shape["sy"]
    nch = KV // nsy
    heads = nsy * GROUP
    np_ = nsx // 2

    def per_device(queries, keys, values, opening, valid, weight):
        tb = queries.shape[0]
        tokens = tb * nsx
        half = tokens // 2
        owners = half // PIECE
        slots = keys.shape[0]
        q = queries.reshape(tb, nsy, nch, GROUP, HEAD).transpose(2, 1, 3, 0, 4)
        q = q.reshape(nch, heads * tb, HEAD)
        columns = weight.shape[1]
        dma = pltpu.SemaphoreType.DMA
        vmem = pl.BlockSpec(memory_space=pltpu.VMEM)
        smem = pl.BlockSpec(memory_space=pltpu.SMEM)
        hbm = pl.BlockSpec(memory_space=pl.ANY)
        return pl.pallas_call(
            functools.partial(kernel, nsx, nsy),
            out_shape=jax.ShapeDtypeStruct((tokens // nsy, columns), BF16),
            in_specs=[vmem, hbm, hbm, smem, smem, hbm],
            out_specs=vmem,
            scratch_shapes=[
                pltpu.VMEM((KV, slots, HEAD), BF16),
                pltpu.VMEM((KV, slots, 2 * HEAD), BF16),
                pltpu.VMEM(weight.shape, BF16),
                pltpu.VMEM((nch, 2, np_, heads * tb, HEAD), BF16),
                pltpu.VMEM((heads, tokens, HEAD), F32),
                pltpu.VMEM((GROUP * tokens, HEAD), BF16),
                pltpu.VMEM((tokens, slots), F32),
                pltpu.VMEM((tokens, HEAD), F32),
                pltpu.VMEM((GROUP * tokens, slots), F32),
                pltpu.VMEM((GROUP * tokens, slots), F32),
                pltpu.VMEM((GROUP * tokens, HEAD), F32),
                pltpu.VMEM((GROUP * tokens, HEAD), F32),
                pltpu.VMEM((GROUP * tokens, HEAD), F32),
                pltpu.VMEM((GROUP * tokens, 2 * HEAD), F32),
                pltpu.VMEM((nch, 2, heads, half, HEAD), BF16),
                pltpu.VMEM((nch, 2, 2, half, HEAD), F32),
                pltpu.VMEM((nch, heads, half, HEAD), BF16),
                pltpu.VMEM((nch, 2, half, HEAD), F32),
                pltpu.VMEM((nch, nsy, owners, ROWS, HEAD), BF16),
                pltpu.VMEM((nch, np_ * nsy, ROWS, HEAD), BF16),
                pltpu.VMEM((nch, 2, owners, ROWS, HEAD), BF16),
                pltpu.VMEM((tokens, GROUP * HEAD), F32),
                pltpu.VMEM((tokens, columns), F32),
                pltpu.VMEM((nsy, tokens // nsy, columns), F32),
                pltpu.VMEM((nsy, tokens // nsy, columns), F32),
                dma((KV,)), dma((KV,)), dma,
            ] + [dma((nch,))] * 14 + [dma, dma],
            compiler_params=pltpu.CompilerParams(
                collective_id=0, has_side_effects=True, vmem_limit_bytes=56 * 1024 * 1024),
        )(q, keys, values, opening, valid, weight)

    return jax.shard_map(
        per_device,
        mesh=mesh,
        in_specs=(
            P("sx", None),
            P(("sx", "sy"), None),
            P(("sx", "sy"), None),
            P(),
            P(("sx", "sy")),
            P("sy", "sx"),
        ),
        out_specs=P("sy", "sx"),
        check_vma=False,
    )
```

```python
import functools
import math

import jax
import jax.numpy as jnp
from jax import lax
from jax.experimental import pallas as pl
from jax.experimental.pallas import tpu as pltpu
from jax.sharding import PartitionSpec as P

HEAD = 128
KV = 8
GROUP = 5
BLOCK = 512
PIECE = 8
ROWS = 48
F32 = jnp.float32
BF16 = jnp.bfloat16
MESH = pl.DeviceIdType.MESH
LOG2E = math.log2(math.e)


def wait_for(ref, sem):
    pltpu.make_async_copy(ref, ref, sem).wait()


def kernel(
    nsx, nsy,
    q_ref, k_hbm, v_hbm, open_ref, valid_ref, w_hbm, out_ref,
    kbuf, vbuf, wbuf, qg, qf, qb, bias, temper, score0, score1, top0, top1, part, oacc, obuf, stat, crecv, cstat,
    dsend, drecv, ag, att, acc, ysend, yrecv,
    ksem, vsem, wsem, qd_s, qd_r, qx_s, qx_r, qc_s, qc_r, c_s, c_r, t_s, t_r,
    d_s, d_r, a_s, a_r, f_s, f_r, y_s, y_r,
):
    np_ = nsx // 2
    nch = KV // nsy
    heads = nsy * GROUP
    tokens = qf.shape[1]
    half = tokens // 2
    slots = kbuf.shape[1]
    owners = half // PIECE
    tb = tokens // nsx
    sx = lax.axis_index("sx")
    sy = lax.axis_index("sy")
    core = lax.rem(sx, 2)
    other = 1 - core
    p = sx // 2
    grp = (p // owners) * owners
    nhi, hi, lo = np_ // 2, p // 2, lax.rem(p, 2)
    lane_p = lax.rem(p, owners)
    partner = {"sx": p * 2 + other, "sy": sy}

    def same_core(i):
        at = lax.rem(sy * np_ + p + i, np_ * nsy)
        return {"sx": lax.rem(at, np_) * 2 + core, "sy": at // np_}, at

    barrier = pltpu.get_barrier_semaphore()

    def greet(i, _):
        dev, _at = same_core(i)
        pl.semaphore_signal(barrier, inc=1, device_id=dev, device_id_type=MESH)
        return 0

    lax.fori_loop(1, np_ * nsy, greet, 0)
    pl.semaphore_signal(barrier, inc=1, device_id=partner, device_id_type=MESH)

    order = [j * nch + c for c in range(nch) for j in range(nsy)]

    def load_k(g):
        return pltpu.make_async_copy(k_hbm.at[:, pl.ds(g * HEAD, HEAD)], kbuf.at[g], ksem.at[g])

    def load_v(g):
        return pltpu.make_async_copy(
            v_hbm.at[:, pl.ds(g * HEAD, HEAD)], vbuf.at[g, :, pl.ds(0, HEAD)], vsem.at[g])

    for g in order:
        load_k(g).start()
        load_v(g).start()
    load_w = pltpu.make_async_copy(w_hbm, wbuf, wsem)
    load_w.start()

    pl.semaphore_wait(barrier, np_ * nsy)

    for c in range(nch):
        qg[c, core, lo, hi] = jnp.concatenate(
            [q_ref[:, pl.ds(((j * nch + c) * GROUP + h) * HEAD, HEAD)].astype(F32)
             for j in range(nsy) for h in range(GROUP)], axis=0).astype(BF16)

    def send_q(c):
        def send(i, _):
            to = lax.rem(hi + i, nhi) * 2 + lo
            pltpu.make_async_remote_copy(
                qg.at[c, core, lo, hi], qg.at[c, core, lo, hi], qd_s.at[c], qd_r.at[c],
                device_id={"sx": to * 2 + core, "sy": sy}, device_id_type=MESH).start()
            return 0
        lax.fori_loop(1, nhi, send, 0)

    send_q(0)

    t_col = lax.broadcasted_iota(jnp.int32, (tokens, 1), 0)
    position = open_ref[0] + t_col
    buckets = lax.shift_right_logical(position + 1, 13).astype(F32)
    temper[...] = jnp.broadcast_to(
        (1.0 + 0.1 * jnp.log(buckets + 1.0)) * (HEAD ** -0.5 * LOG2E), temper.shape)
    limit = jnp.minimum(valid_ref[0], position + 1 - (sx * nsy + sy) * slots)
    bias[...] = jnp.where(
        lax.broadcasted_iota(jnp.int32, (tokens, slots), 1) < limit, 0.0, -1e30).astype(F32)

    def ones(g, _):
        vbuf[g, :, HEAD:] = jnp.ones((slots, HEAD), BF16)
        return 0
    lax.fori_loop(0, KV, ones, 0)
    acc[...] = jnp.zeros_like(acc)

    def spread_q(c):
        wait_for(qg.at[c, 0, 0, pl.ds(0, nhi - 1)], qd_r.at[c])
        pltpu.make_async_remote_copy(
            qg.at[c, core, lo], qg.at[c, core, lo], qx_s.at[c], qx_r.at[c],
            device_id={"sx": (hi * 2 + 1 - lo) * 2 + core, "sy": sy}, device_id_type=MESH).start()

    def forward_q(c):
        wait_for(qg.at[c, 0, 0], qx_r.at[c])
        pltpu.make_async_remote_copy(
            qg.at[c, core], qg.at[c, core], qc_s.at[c], qc_r.at[c],
            device_id=partner, device_id_type=MESH).start()

    def take_q(c):
        wait_for(qg.at[c, 0], qc_r.at[c])

        def place(i, _):
            x0 = qg[c, 0, lax.rem(i, 2), i // 2].astype(F32)
            x1 = qg[c, 1, lax.rem(i, 2), i // 2].astype(F32)
            at = pl.multiple_of(i * 2 * tb, 2 * tb)
            for k in range(heads):
                qf[k, pl.ds(at, 2 * tb), :] = jnp.concatenate(
                    [x0[k * tb:(k + 1) * tb], x1[k * tb:(k + 1) * tb]], axis=0)
            return 0
        lax.fori_loop(0, np_, place, 0)
        stat[c, :, 0] = jnp.full((2, half, HEAD), -1e29, F32)
        stat[c, :, 1] = jnp.zeros((2, half, HEAD), F32)

    scores, tops = (score0, score1), (top0, top1)

    def wide(x):
        return jnp.concatenate([x] * (BLOCK // HEAD), axis=1)

    def step(cur, nxt):
        if nxt is not None:
            g = order[nxt]
            load_k(g).wait()
            first = (nxt % nsy) * GROUP
            for h in range(GROUP):
                qb[pl.ds(h * tokens, tokens), :] = qf[first + h].astype(BF16)
            part[...] = jnp.full(part.shape, -1e29, F32)
        if cur is not None:
            load_v(order[cur]).wait()
            oacc[...] = jnp.zeros_like(oacc)

        def block(n, _):
            at = pl.multiple_of(n * BLOCK, BLOCK)
            keys = pl.ds(at, BLOCK)
            if nxt is not None:
                s = lax.dot_general(qb[...], kbuf[order[nxt], keys, :], (((1,), (1,)), ((), ())),
                                    preferred_element_type=F32)
                scale, hide = wide(temper[...]), bias[:, keys]
                for h in range(GROUP):
                    rows = slice(h * tokens, (h + 1) * tokens)
                    x = s[rows] * scale + hide
                    scores[nxt % 2][rows, keys] = x
                    m = part[rows, :]
                    for i in range(BLOCK // HEAD):
                        m = jnp.maximum(m, x[:, i * HEAD:(i + 1) * HEAD])
                    part[rows, :] = m
            if cur is not None:
                w = jnp.exp2(scores[cur % 2][:, keys] - wide(tops[cur % 2][...])).astype(BF16)
                oacc[...] += jnp.dot(w, vbuf[order[cur], keys, :], preferred_element_type=F32)
            return 0
        lax.fori_loop(0, slots // BLOCK, block, 0)

        if nxt is not None:
            tops[nxt % 2][...] = jnp.broadcast_to(
                jnp.max(part[...], axis=1, keepdims=True), part.shape)
        if cur is not None:
            c = cur // nsy
            lane = lax.broadcasted_iota(jnp.int32, (half, HEAD), 1)
            for b in range(2):
                m, l = stat[c, b, 0], stat[c, b, 1]
                for h in range(GROUP):
                    k = (cur % nsy) * GROUP + h
                    rows = pl.ds(h * tokens + b * half, half)
                    obuf[c, b, k] = oacc[rows, :HEAD].astype(BF16)
                    m = jnp.where(lane == k, tops[cur % 2][rows, :], m)
                    l = jnp.where(lane == k, oacc[rows, HEAD:], l)
                stat[c, b, 0], stat[c, b, 1] = m, l

    def pair_copies(c):
        return (
            pltpu.make_async_remote_copy(
                obuf.at[c, other], crecv.at[c], c_s.at[c], c_r.at[c],
                device_id=partner, device_id_type=MESH),
            pltpu.make_async_remote_copy(
                stat.at[c, other], cstat.at[c], t_s.at[c], t_r.at[c],
                device_id=partner, device_id_type=MESH))

    def send_pair(c):
        for copy in pair_copies(c):
            copy.start()

    def send_owners(c):
        for copy in pair_copies(c):
            copy.wait_recv()
        m0, m1 = stat[c, core, 0], cstat[c, 0]
        m = jnp.maximum(m0, m1)
        f0, f1 = jnp.exp2(m0 - m), jnp.exp2(m1 - m)
        l = stat[c, core, 1] * f0 + cstat[c, 1] * f1
        terms = []
        for x, n in ((m, 3), (l, 2)):
            for _ in range(n):
                terms.append(x.astype(BF16).astype(F32))
                x = x - terms[-1]
        lane = lax.broadcasted_iota(jnp.int32, (half, HEAD), 1)
        for j in range(nsy):
            def turn(x, by):
                by = by % HEAD
                return pltpu.roll(x, by, 1) if by else x
            st = turn(terms[0], -GROUP * j)
            for i in range(1, len(terms)):
                st = jnp.where(lane < 8 * i, st, turn(terms[i], 8 * i - GROUP * j))
            parts = []
            for h in range(GROUP):
                k = j * GROUP + h
                parts.append(obuf[c, core, k].astype(F32) * f0[:, k:k + 1]
                             + crecv[c, k].astype(F32) * f1[:, k:k + 1])
            parts.append(st)
            for o in range(owners):
                rows = slice(o * PIECE, (o + 1) * PIECE)
                dsend[c, j, o] = jnp.concatenate([x[rows] for x in parts], axis=0).astype(BF16)
        here = sy * np_ + p
        drecv[c, here] = dsend[c, sy, lane_p]

        def send(i, _):
            dev, at = same_core(i)
            pltpu.make_async_remote_copy(
                dsend.at[c, at // np_, lax.rem(at, owners)], drecv.at[c, here], d_s.at[c], d_r.at[c],
                device_id=dev, device_id_type=MESH).start()
            return 0
        lax.fori_loop(1, np_ * nsy, send, 0)

    def send_attended(c):
        n = np_ * nsy
        wait_for(drecv.at[c, pl.ds(0, n - 1)], d_r.at[c])
        first = GROUP * PIECE

        def join(st, *at):
            return sum(pltpu.roll(st, HEAD - 8 * i, 1) for i in at)

        def largest(i, m):
            st = drecv[c, i].astype(F32)[first:]
            return jnp.maximum(m, st + join(st, 1, 2))
        m = lax.fori_loop(0, n, largest, jnp.full((PIECE, HEAD), -1e29, F32))

        def add(i, carry):
            x = drecv[c, i].astype(F32)
            st = x[first:]
            f = jnp.exp2(st + join(st, 1, 2) - m)
            l = join(st, 3, 4)
            outs = tuple(
                a + f[:, h:h + 1] * x[h * PIECE:(h + 1) * PIECE] for h, a in enumerate(carry[1:]))
            return (carry[0] + f * l,) + outs
        zero = jnp.zeros((PIECE, HEAD), F32)
        total, *outs = lax.fori_loop(0, n, add, (zero,) * (GROUP + 1))
        outs = [o / total[:, h:h + 1] for h, o in enumerate(outs)]
        ag[c, core, lane_p] = jnp.concatenate(outs + [zero], axis=0).astype(BF16)

        def send(i, _):
            to = grp + lax.rem(lane_p + i, owners)
            pltpu.make_async_remote_copy(
                ag.at[c, core, lane_p], ag.at[c, core, lane_p], a_s.at[c], a_r.at[c],
                device_id={"sx": to * 2 + core, "sy": sy}, device_id_type=MESH).start()
            return 0
        lax.fori_loop(1, owners, send, 0)

    def forward_attended(c):
        wait_for(ag.at[c, 0, pl.ds(0, owners - 1)], a_r.at[c])
        pltpu.make_async_remote_copy(
            ag.at[c, core], ag.at[c, core], f_s.at[c], f_r.at[c],
            device_id=partner, device_id_type=MESH).start()

    def project(c):
        wait_for(ag.at[c, 0], f_r.at[c])
        if c == 0:
            load_w.wait()
        for b in range(2):
            for o in range(owners):
                x = ag[c, b, o].astype(F32)
                for h in range(GROUP):
                    att[pl.ds(b * half + o * PIECE, PIECE), pl.ds(h * HEAD, HEAD)] = (
                        x[h * PIECE:(h + 1) * PIECE])
        width = GROUP * HEAD
        acc[...] += lax.dot_general(
            att[...].astype(BF16), wbuf[:, pl.ds(c * width, width)], (((1,), (1,)), ((), ())),
            preferred_element_type=F32)

    stages = (send_pair, send_owners, send_attended, forward_attended, project)
    spread_q(0)
    if nch > 1:
        send_q(1)
    forward_q(0)
    take_q(0)
    if nch > 1:
        spread_q(1)
    step(None, 0)
    for i in range(KV + len(stages) - 1):
        if i % nsy == 0 and i // nsy + 1 < nch:
            forward_q(i // nsy + 1)
        if i % nsy == 0 and i // nsy + 2 < nch:
            send_q(i // nsy + 2)
        if (i + 1) % nsy == 0 and (i + 1) // nsy < nch:
            take_q((i + 1) // nsy)
            if (i + 1) // nsy + 1 < nch:
                spread_q((i + 1) // nsy + 1)
        if i < KV:
            step(i, i + 1 if i + 1 < KV else None)
        for s, stage in enumerate(stages):
            done = i + 1 - s
            if done % nsy == 0 and 0 < done <= KV:
                stage(done // nsy - 1)

    block = tokens // nsy
    for j in range(nsy):
        ysend[j] = acc[j * block:(j + 1) * block, :]

    def send_y(i, _):
        to = lax.rem(sy + i, nsy)
        pltpu.make_async_remote_copy(
            ysend.at[to], yrecv.at[sy], y_s, y_r,
            device_id={"sx": sx, "sy": to}, device_id_type=MESH).start()
        return 0
    lax.fori_loop(1, nsy, send_y, 0)
    yrecv[sy] = ysend[sy]
    wait_for(yrecv.at[pl.ds(0, nsy - 1)], y_r)
    total = yrecv[0]
    for j in range(1, nsy):
        total = total + yrecv[j]
    out_ref[...] = total.astype(BF16)

    wait_for(ysend.at[pl.ds(0, nsy - 1)], y_s)
    for c in range(nch):
        wait_for(qg.at[c, 0, 0, pl.ds(0, nhi - 1)], qd_s.at[c])
        wait_for(qg.at[c, 0, 0], qx_s.at[c])
        wait_for(qg.at[c, 0], qc_s.at[c])
        for copy in pair_copies(c):
            copy.wait_send()
        wait_for(drecv.at[c, pl.ds(0, np_ * nsy - 1)], d_s.at[c])
        wait_for(ag.at[c, 0, pl.ds(0, owners - 1)], a_s.at[c])
        wait_for(ag.at[c, 0], f_s.at[c])


def solution(mesh):
    nsx, nsy = mesh.shape["sx"], mesh.shape["sy"]
    nch = KV // nsy
    heads = nsy * GROUP
    np_ = nsx // 2

    def per_device(queries, keys, values, opening, valid, weight):
        tb = queries.shape[0]
        tokens = tb * nsx
        half = tokens // 2
        owners = half // PIECE
        slots = keys.shape[0]
        columns = weight.shape[1]
        dma = pltpu.SemaphoreType.DMA
        vmem = pl.BlockSpec(memory_space=pltpu.VMEM)
        smem = pl.BlockSpec(memory_space=pltpu.SMEM)
        hbm = pl.BlockSpec(memory_space=pl.ANY)
        return pl.pallas_call(
            functools.partial(kernel, nsx, nsy),
            out_shape=jax.ShapeDtypeStruct((tokens // nsy, columns), BF16),
            in_specs=[vmem, hbm, hbm, smem, smem, hbm],
            out_specs=vmem,
            scratch_shapes=[
                pltpu.VMEM((KV, slots, HEAD), BF16),
                pltpu.VMEM((KV, slots, 2 * HEAD), BF16),
                pltpu.VMEM(weight.shape[::-1], BF16),
                pltpu.VMEM((nch, 2, 2, np_ // 2, heads * tb, HEAD), BF16),
                pltpu.VMEM((heads, tokens, HEAD), F32),
                pltpu.VMEM((GROUP * tokens, HEAD), BF16),
                pltpu.VMEM((tokens, slots), F32),
                pltpu.VMEM((tokens, HEAD), F32),
                pltpu.VMEM((GROUP * tokens, slots), F32),
                pltpu.VMEM((GROUP * tokens, slots), F32),
                pltpu.VMEM((GROUP * tokens, HEAD), F32),
                pltpu.VMEM((GROUP * tokens, HEAD), F32),
                pltpu.VMEM((GROUP * tokens, HEAD), F32),
                pltpu.VMEM((GROUP * tokens, 2 * HEAD), F32),
                pltpu.VMEM((nch, 2, heads, half, HEAD), BF16),
                pltpu.VMEM((nch, 2, 2, half, HEAD), F32),
                pltpu.VMEM((nch, heads, half, HEAD), BF16),
                pltpu.VMEM((nch, 2, half, HEAD), F32),
                pltpu.VMEM((nch, nsy, owners, ROWS, HEAD), BF16),
                pltpu.VMEM((nch, np_ * nsy, ROWS, HEAD), BF16),
                pltpu.VMEM((nch, 2, owners, ROWS, HEAD), BF16),
                pltpu.VMEM((tokens, GROUP * HEAD), F32),
                pltpu.VMEM((tokens, columns), F32),
                pltpu.VMEM((nsy, tokens // nsy, columns), F32),
                pltpu.VMEM((nsy, tokens // nsy, columns), F32),
                dma((KV,)), dma((KV,)), dma,
            ] + [dma((nch,))] * 16 + [dma, dma],
            compiler_params=pltpu.CompilerParams(
                collective_id=0, has_side_effects=True, vmem_limit_bytes=56 * 1024 * 1024),
        )(queries, keys, values, opening, valid, weight.T)

    return jax.shard_map(
        per_device,
        mesh=mesh,
        in_specs=(
            P("sx", None),
            P(("sx", "sy"), None),
            P(("sx", "sy"), None),
            P(),
            P(("sx", "sy")),
            P("sy", "sx"),
        ),
        out_specs=P("sy", "sx"),
        check_vma=False,
    )
```
